512 devices in a mesh: node: 16 (over z, core), local: 32 (over y, x).
Axes of the slice: x: 4, y: 8, z: 8, core: 2. Of those that a mesh axis runs over, the one named last changes fastest.
Arguments:
- tokens: bfloat16 [8192, 2048], P(('node', 'local')), may hold values from -6 to 6
- grad_out: bfloat16 [8192, 2048], P(('node', 'local')), may hold values from -6 to 6
- expert_ids: int32 [8192, 8], P(('node', 'local')), may hold values from 0 to 127, all different within a row; in each aligned block of 16 rows (0 to 15, 16 to 31, ...) at most 2 rows name the same one
- scores: bfloat16 [8192, 8], P(('node', 'local')), may hold values from 0.049804688 to 0.5
- gate_weight: bfloat16 [16, 32, 192, 2048], P('node', 'local'), may hold values from -0.125 to 0.125
- up_weight: bfloat16 [16, 32, 192, 2048], P('node', 'local'), may hold values from -0.125 to 0.125
- down_weight: bfloat16 [16, 32, 192, 2048], P('node', 'local'), may hold values from -0.21875 to 0.21875
Outputs:
- d_tokens: bfloat16 [8192, 2048], P(('node', 'local'))
- d_scores: bfloat16 [8192, 8], P(('node', 'local'))
- d_gate_weight: bfloat16 [16, 32, 192, 2048], P('node', 'local')
- d_up_weight: bfloat16 [16, 32, 192, 2048], P('node', 'local')
- d_down_weight: bfloat16 [16, 32, 192, 2048], P('node', 'local')
The draws below stay inside these ranges and needn't reach their ends.
Inputs may be any that keep to these rules, and one draw needn't show every extreme that they name: `expert_ids`: each row names 8 different experts. Among the 16 rows of one device (aligned blocks of rows) no expert is named more than 2 times, and in every draw some expert is named exactly 2 times in some block.
All inputs are finite; a program needn't handle non-finite values.
Results may differ from the reference program's by a relative error of at most 0.017.
Values may be sent and summed in bfloat16 or wider, within the bound.
No kernel may reach another device: no remote copies, remote signals or barrier semaphores. Data moves between devices by JAX's collectives and lax.ppermute only.
A program may use at most 64 MiB of HBM per device.

```python
import math
import jax
import jax.numpy as jnp
import numpy as np
from jax import lax

D = 2048
FF = 768
TOP = 8
TOK_DEV = 16
EXPERTS = 128
SHARDS = 4
FF_DEV = 192
CAP = 2
TOKENS = 8192
N_NODE = 16
N_LOCAL = 32


def level_of(key, extent, cuts, smallest, top_value):
    level = 1.0
    for position, shards_of in cuts:
        steps = jax.random.uniform(jax.random.fold_in(jax.random.fold_in(key, 6), position), (shards_of,), jnp.float32, smallest / len(cuts), top_value / len(cuts))
        level = level * jnp.repeat(jnp.exp(steps), extent[position] // shards_of).reshape((-1,) + (1,) * (len(extent) - 1 - position))
    return level


def routed_block(key, own, number, rows, number_of, top, bound, skew):
    ranking = jax.random.permutation(key, number_of)
    heavy_load, usual = load_shares(number_of, rows * top, bound, skew, True), load_shares(number_of, rows * top, bound, skew, False)
    places = jnp.arange(number_of)

    def named(sizes, rotation):
        used = int((sizes > 0).sum())
        fixed = max(1, used // 4)
        passed = fixed + (places - fixed + rotation * (used - fixed)) % max(1, number_of - fixed)
        return jnp.zeros((number_of,), jnp.int32).at[ranking[jnp.where(places < fixed, places, passed)]].set(jnp.asarray(sizes, jnp.int32))

    sizes = jnp.where(number % 4 == 0, named(heavy_load, number // 4), named(usual, number - number // 4 - 1))
    mixed = jax.random.permutation(jax.random.fold_in(own, 3), number_of)
    giver, sink = mixed[0:number_of // 2 * 2:2], mixed[1:number_of // 2 * 2:2]
    slack = jnp.minimum(sizes[giver] - 1, bound - sizes[sink]) // 2
    slack = jnp.where((giver == ranking[0]) | (sink == ranking[0]) | (sizes[sink] == 0), 0, jnp.maximum(slack, 0))
    passed = jax.random.randint(jax.random.fold_in(own, 4), (number_of // 2,), 0, 1 << 20) % (slack + 1)
    sizes = sizes.at[giver].add(-passed).at[sink].add(passed)
    members = jnp.searchsorted(jnp.cumsum(sizes), jnp.arange(rows * top), side="right").astype(jnp.int32)
    grid = members.reshape(top, rows).T
    grid = grid[jax.random.permutation(jax.random.fold_in(own, 1), rows)]
    rotation = jax.random.randint(jax.random.fold_in(own, 2), (rows, 1), 0, top)
    return jnp.take_along_axis(grid, (jnp.arange(top)[None, :] + rotation) % top, axis=1)


def load_shares(number_of, total, reach, slope, full):
    loads = [(1 << 20) // math.isqrt(grade ** slope) + 1 for grade in range(1, number_of + 1)]
    largest = reach if full else min(reach, max(-(-total // number_of), total * loads[0] // sum(loads)))
    least = 1 if total - largest >= number_of - 1 else 0
    counts, surplus = [largest] + [least] * (number_of - 1), total - largest - least * (number_of - 1)
    while surplus > 0:
        free = [i for i in range(1, number_of) if counts[i] < largest] or [i for i in range(1, number_of) if counts[i] < reach]
        pool, budget = sum([loads[i] for i in free]), surplus
        for i in free:
            more = min(reach - counts[i], max(1, budget * loads[i] // pool), surplus)
            counts[i] = counts[i] + more
            surplus = surplus - more
    return np.array(counts)


def bell_draw(key, dims, deviation, limit, split=(), kind=jnp.bfloat16):
    array = jax.random.normal(key, dims, jnp.float32) * deviation
    if len(split) > 0:
        array = level_of(key, dims, split, -0.22, 0.18) * array
    return jnp.clip(array, min=-limit, max=limit).astype(kind)


def setup_inputs(seed: int = 0) -> dict:
    arg_keys = jax.random.split(jax.random.key(seed), 8)
    tokens = bell_draw(arg_keys[0], (TOKENS, D), 1.0, 6.0, ((0, 512),))
    grad_out = bell_draw(arg_keys[1], (TOKENS, D), 1.0, 6.0, ((0, 512),))
    expert_ids_keys = jax.random.split(jax.random.fold_in(arg_keys[2], 1), TOKENS // TOK_DEV)
    expert_ids_turns = jax.random.permutation(jax.random.fold_in(arg_keys[2], 3), TOKENS // TOK_DEV)
    expert_ids = jax.vmap(lambda own, number: routed_block(jax.random.fold_in(arg_keys[2], 2), own, number, TOK_DEV, EXPERTS, TOP, CAP, 2))(expert_ids_keys, expert_ids_turns).reshape((TOKENS, TOP))
    scores = jnp.clip(jnp.exp(math.log(0.5) - 2.306499 * jax.random.uniform(arg_keys[3], (TOKENS, TOP), jnp.float32) ** level_of(arg_keys[3], (TOKENS, TOP), ((0, 512),), -0.2, 0.2)), 0.049804688, 0.5).astype(jnp.bfloat16)
    gate_weight = bell_draw(arg_keys[4], (N_NODE, N_LOCAL, FF_DEV, D), D ** -0.5, 0.125, ((0, 16), (1, 32)))
    up_weight = bell_draw(arg_keys[5], (N_NODE, N_LOCAL, FF_DEV, D), D ** -0.5, 0.125, ((0, 16), (1, 32)))
    down_weight = bell_draw(arg_keys[6], (N_NODE, N_LOCAL, FF_DEV, D), FF ** -0.5, 0.21875, ((0, 16), (1, 32)))
    return dict(tokens=tokens, grad_out=grad_out, expert_ids=expert_ids, scores=scores, gate_weight=gate_weight, up_weight=up_weight, down_weight=down_weight)


def build_slots(expert_ids):
    device_count = N_NODE * N_LOCAL
    flat_ids = expert_ids.reshape(device_count, TOK_DEV * TOP)
    expert_iota = jnp.arange(EXPERTS, dtype=jnp.int32)

    def rank_block(block_ids):
        matches = (block_ids[:, None] == expert_iota[None, :]).astype(jnp.int32)
        earlier = jnp.cumsum(matches, axis=0) - matches
        return jnp.sum(earlier * matches, axis=1).astype(jnp.int32)

    rank_within = lax.map(rank_block, flat_ids)
    device_index = jnp.arange(device_count, dtype=jnp.int32)[:, None]
    slot_index = flat_ids * (device_count * CAP) + device_index * CAP + rank_within
    entries = jnp.arange(TOKENS * TOP, dtype=jnp.int32)
    slot_table = jnp.full((EXPERTS * device_count * CAP,), TOKENS * TOP, jnp.int32)
    slot_table = slot_table.at[slot_index.reshape(-1)].set(entries)
    return slot_table.reshape(EXPERTS, device_count * CAP)


def reference(tokens, grad_out, expert_ids, scores, gate_weight, up_weight, down_weight):
    slot_table = build_slots(expert_ids)
    gate_blocks = gate_weight.reshape(EXPERTS, SHARDS, FF_DEV, D)
    up_blocks = up_weight.reshape(EXPERTS, SHARDS, FF_DEV, D)
    down_blocks = down_weight.reshape(EXPERTS, SHARDS, FF_DEV, D)
    flat_scores = scores.reshape(-1)

    def expert_step(carry, inputs):
        grad_sum, score_grad = carry
        row_entries, w_gate, w_up, w_down = inputs
        usable = row_entries < TOKENS * TOP
        safe_rows = jnp.where(usable, row_entries, 0)
        token_rows = safe_rows // TOP
        x_rows = jnp.where(usable[:, None], tokens[token_rows], 0).astype(jnp.float32)
        dy_rows = jnp.where(usable[:, None], grad_out[token_rows], 0).astype(jnp.float32)
        s_rows = jnp.where(usable, flat_scores[safe_rows], 0).astype(jnp.float32)
        gate_f = w_gate.astype(jnp.float32)
        up_f = w_up.astype(jnp.float32)
        down_f = w_down.astype(jnp.float32)
        pre_gate = jnp.einsum('rd,sfd->srf', x_rows, gate_f)
        pre_up = jnp.einsum('rd,sfd->srf', x_rows, up_f)
        logistic = jax.nn.sigmoid(pre_gate)
        act = (pre_gate * logistic * pre_up).astype(jnp.bfloat16)
        back = jnp.einsum('rd,sfd->srf', dy_rows, down_f)
        act_f = act.astype(jnp.float32)
        score_blocks = jnp.sum(act_f * back, axis=2).astype(jnp.bfloat16)
        score_blocks = lax.optimization_barrier(score_blocks)
        score_rows = jnp.sum(score_blocks.astype(jnp.float32), axis=0).astype(jnp.bfloat16)
        scaled = (s_rows[:, None] * dy_rows).astype(jnp.bfloat16)
        d_act = s_rows[None, :, None] * back
        d_pre_gate = (d_act * pre_up * logistic * (1.0 + pre_gate * (1.0 - logistic))).astype(jnp.bfloat16)
        d_pre_up = (d_act * pre_gate * logistic).astype(jnp.bfloat16)
        dpg_f = d_pre_gate.astype(jnp.float32)
        dpu_f = d_pre_up.astype(jnp.float32)
        partial_rows = (jnp.einsum('srf,sfd->srd', dpg_f, gate_f) + jnp.einsum('srf,sfd->srd', dpu_f, up_f)).astype(jnp.bfloat16)
        partial_rows = lax.optimization_barrier(partial_rows)
        slot_grad = jnp.sum(partial_rows.astype(jnp.float32), axis=0).astype(jnp.bfloat16)
        grad_sum = grad_sum.at[token_rows].add(jnp.where(usable[:, None], slot_grad.astype(jnp.float32), 0.0))
        score_grad = score_grad.at[row_entries].set(score_rows.astype(jnp.float32))
        d_gate = jnp.einsum('srf,rd->sfd', dpg_f, x_rows).astype(jnp.bfloat16)
        d_up = jnp.einsum('srf,rd->sfd', dpu_f, x_rows).astype(jnp.bfloat16)
        d_down = jnp.einsum('srf,rd->sfd', act_f, scaled.astype(jnp.float32)).astype(jnp.bfloat16)
        return (grad_sum, score_grad), (d_gate, d_up, d_down)

    start = (jnp.zeros((TOKENS, D), jnp.float32), jnp.zeros((TOKENS * TOP + 1,), jnp.float32))
    (grad_sum, score_grad), (d_gate, d_up, d_down) = lax.scan(expert_step, start, (slot_table, gate_blocks, up_blocks, down_blocks))
    d_tokens = grad_sum.astype(jnp.bfloat16)
    d_scores = score_grad[:TOKENS * TOP].reshape(TOKENS, TOP).astype(jnp.bfloat16)
    d_gate_weight = d_gate.reshape(N_NODE, N_LOCAL, FF_DEV, D)
    d_up_weight = d_up.reshape(N_NODE, N_LOCAL, FF_DEV, D)
    d_down_weight = d_down.reshape(N_NODE, N_LOCAL, FF_DEV, D)
    return (d_tokens, d_scores, d_gate_weight, d_up_weight, d_down_weight)
```

```python
import functools

import jax
import jax.numpy as jnp
from jax import lax
from jax.experimental import pallas as pl
from jax.experimental.pallas import tpu as pltpu
from jax.sharding import Mesh
from jax.sharding import PartitionSpec as P

TOP = 8
EXP_NODE = 8
CAP = 2
LANES = 128
SUBLANES = 8
VMEM_BYTES = 40 << 20
FLOPS_TOTAL = 0

COLS = (((1,), (1,)), ((), ()))
ROWS = (((0,), (0,)), ((), ()))
PLAIN = (((1,), (0,)), ((), ()))


def dot(a, b, dims):
    return lax.dot_general(a, b, dims, preferred_element_type=jnp.float32)


def right(part, ring):
    return lax.ppermute(part, "block", [(i, (i + 1) % ring) for i in range(ring)])


def left(part, ring):
    return lax.ppermute(part, "block", [(i, (i - 1) % ring) for i in range(ring)])


def on_core(body, outs, flops, *operands):
    size = sum(v.size * v.dtype.itemsize for v in (*operands, *outs))
    return pl.pallas_call(
        body,
        out_shape=outs,
        in_specs=[pl.BlockSpec(memory_space=pltpu.VMEM)] * len(operands),
        out_specs=[pl.BlockSpec(memory_space=pltpu.VMEM)] * len(outs),
        compiler_params=pltpu.CompilerParams(vmem_limit_bytes=VMEM_BYTES),
        cost_estimate=pl.CostEstimate(flops=int(flops), bytes_accessed=size, transcendentals=0),
    )(*operands)


def halves(refs):
    if len(refs) == 2:
        return [ref[...] for ref in refs]
    half = refs[0].shape[1] // 2
    return [refs[0][:, :half], refs[0][:, half:]]


def prepare_body(width, rows_ref, scaled_ref, s_ref):
    s_lanes = rows_ref[:, 2 * width :].astype(jnp.float32)
    dy = rows_ref[:, width : 2 * width].astype(jnp.float32)
    scaled_ref[...] = (s_lanes[:, :1] * dy).astype(jnp.bfloat16)
    s_ref[...] = s_lanes.T[:SUBLANES]


def block_body(width, units, parts, rows_ref, scaled_ref, s_ref, *refs):
    weights, (grad_a, grad_b, d_pre_ref, d_s_ref) = halves(refs[:parts]), refs[parts:]
    half = width // 2
    x = [rows_ref[:, :half], rows_ref[:, half:width]]
    dy = [rows_ref[:, width : width + half], rows_ref[:, width + half : 2 * width]]
    pre = sum(dot(w[: 2 * units], v, COLS) for w, v in zip(weights, x))
    back = sum(dot(w[2 * units :], v, COLS) for w, v in zip(weights, dy))
    pre_gate, pre_up = pre[:units], pre[units:]
    logistic = 1.0 / (1.0 + jnp.exp(-pre_gate))
    act = (pre_gate * logistic * pre_up).astype(jnp.bfloat16)
    d_s = jnp.sum(act.astype(jnp.float32) * back, axis=0, keepdims=True)
    d_s_ref[...] = jnp.broadcast_to(d_s, d_s_ref.shape)
    d_act = s_ref[:1] * back
    d_gate = d_act * pre_up * logistic * (1.0 + pre_gate * (1.0 - logistic))
    d_up = d_act * pre_gate * logistic
    d_pre = jnp.concatenate([d_gate, d_up], axis=0)
    d_pre_ref[...] = d_pre.T.astype(jnp.bfloat16)
    d_pre = d_pre.astype(jnp.bfloat16)
    for i, grad in enumerate((grad_a, grad_b)):
        grad[: 2 * units] = dot(d_pre, x[i], PLAIN).astype(grad.dtype)
        grad[2 * units :] = dot(
            act, scaled_ref[:, i * half : (i + 1) * half], PLAIN
        ).astype(grad.dtype)


def input_body(width, units, parts, *refs):
    count = len(parts)
    d_pre, d_s, refs = refs[:count], refs[count : 2 * count], refs[2 * count :]
    weights, at = [], 0
    for part in parts:
        weights.append(halves(refs[at : at + part]))
        at += part
    out_ref = refs[at]
    half = width // 2
    for i in range(2):
        total = sum(dot(d_pre[b][...], weights[b][i][: 2 * units], PLAIN) for b in range(count))
        out_ref[:, i * half : (i + 1) * half] = total.astype(jnp.bfloat16)
    scores = sum(ref[...] for ref in d_s)[:1]
    scores = jnp.broadcast_to(scores, (LANES, scores.shape[1])).T
    out_ref[:, width:] = scores.astype(jnp.bfloat16)


def total_body(units, mine_a, mine_b, left_a, left_b, right_a, right_b, *outs):
    half = mine_a.shape[1]
    for j, out in enumerate(outs):
        rows = slice(j * units, (j + 1) * units)
        for i, three in enumerate(((mine_a, left_a, right_a), (mine_b, left_b, right_b))):
            out[:, i * half : (i + 1) * half] = sum(
                ref[rows].astype(jnp.float32) for ref in three
            ).astype(jnp.bfloat16)


def on_device(tokens, grad_out, expert_ids, scores, gate_weight, up_weight, down_weight):
    ring = lax.axis_size("block")
    expert_count = lax.axis_size("node") * lax.axis_size("expert")
    tok_count, width = tokens.shape
    units = gate_weight.shape[2]
    half = width // 2
    slot_count = expert_count * CAP
    bf16, f32 = jnp.bfloat16, jnp.float32
    shape = jax.ShapeDtypeStruct

    own = jnp.concatenate([gate_weight[0, 0], up_weight[0, 0], down_weight[0, 0]], axis=0)
    before = right(own, ring)
    after = left(own, ring)
    far_a = right(before[:, :half], ring)
    far_b = left(after[:, half:], ring)

    flat_ids = expert_ids.reshape(-1)
    expert_iota = jnp.arange(expert_count, dtype=jnp.int32)
    matches = (flat_ids[:, None] == expert_iota[None, :]).astype(jnp.int32)
    rank_within = jnp.sum((jnp.cumsum(matches, axis=0) - matches) * matches, axis=1)
    slot_index = flat_ids * CAP + rank_within
    placed = jnp.arange(slot_count, dtype=jnp.int32)[:, None] == slot_index[None, :]
    token_map = placed.reshape(slot_count, tok_count, TOP).sum(axis=2).astype(bf16)
    rows = dot(token_map, jnp.concatenate([tokens, grad_out], axis=1), PLAIN)
    slot_s = jnp.sum(jnp.where(placed, scores.reshape(-1)[None, :], 0), axis=1)
    outgoing = jnp.concatenate(
        [rows.astype(bf16), jnp.broadcast_to(slot_s[:, None], (slot_count, LANES))], axis=1
    )
    rows = lax.all_to_all(
        outgoing.reshape(expert_count, CAP, 2 * width + LANES), ("node", "expert"), 0, 0, tiled=True
    ).reshape(slot_count, 2 * width + LANES)
    scaled, s_rows = on_core(
        functools.partial(prepare_body, width),
        [shape((slot_count, width), bf16), shape((SUBLANES, slot_count), f32)],
        0,
        rows,
    )

    def block(weights, kinds):
        return on_core(
            functools.partial(block_body, width, units, len(weights)),
            [
                shape((3 * units, half), kinds[0]),
                shape((3 * units, half), kinds[1]),
                shape((slot_count, 2 * units), bf16),
                shape((SUBLANES, slot_count), f32),
            ],
            12 * slot_count * units * width,
            rows,
            scaled,
            s_rows,
            *weights,
        )

    blocks = ((far_a, far_b), (after,), (before,), (own,))
    far = block(blocks[0], (bf16, bf16))
    passing_a = right(far[0], ring)
    passing_b = left(far[1], ring)
    nxt = block(blocks[1], (f32, bf16))
    prev = block(blocks[2], (bf16, f32))
    left_b = right(nxt[1], ring)
    right_a = left(prev[0], ring)
    left_a = right((nxt[0] + passing_a.astype(f32)).astype(bf16), ring)
    right_b = left((prev[1] + passing_b.astype(f32)).astype(bf16), ring)
    mine = block(blocks[3], (f32, f32))
    d_gate, d_up, d_down = on_core(
        functools.partial(total_body, units),
        [shape((units, width), bf16)] * 3,
        FLOPS_TOTAL,
        *mine[:2],
        left_a,
        left_b,
        right_a,
        right_b,
    )

    terms = (far, nxt, prev, mine)
    (returning,) = on_core(
        functools.partial(input_body, width, units, [len(w) for w in blocks]),
        [shape((slot_count, width + LANES), bf16)],
        16 * slot_count * units * width,
        *[t[2] for t in terms],
        *[t[3] for t in terms],
        *[w for ws in blocks for w in ws],
    )
    home = lax.all_to_all(
        returning.reshape(expert_count, CAP, width + LANES), ("node", "expert"), 0, 0, tiled=True
    ).reshape(slot_count, width + LANES)
    d_tokens = dot(token_map, home[:, :width], ROWS).astype(bf16)
    d_scores = (
        jnp.sum(jnp.where(placed, home[:, width].astype(f32)[:, None], 0.0), axis=0)
        .reshape(tok_count, TOP)
        .astype(bf16)
    )
    return (d_tokens, d_scores, d_gate[None, None], d_up[None, None], d_down[None, None])


def solution(mesh):
    node_count, local_count = mesh.devices.shape
    mesh = Mesh(
        mesh.devices.reshape(node_count, EXP_NODE, local_count // EXP_NODE),
        ("node", "expert", "block"),
    )
    by_token = P(("node", "expert", "block"), None)
    by_block = P("node", ("expert", "block"), None, None)
    return jax.shard_map(
        on_device,
        mesh=mesh,
        in_specs=(by_token,) * 4 + (by_block,) * 3,
        out_specs=(by_token,) * 2 + (by_block,) * 3,
        check_vma=False,
    )
```

```python
import functools

import jax
import jax.numpy as jnp
from jax import lax
from jax.experimental import pallas as pl
from jax.experimental.pallas import tpu as pltpu
from jax.sharding import Mesh
from jax.sharding import PartitionSpec as P

TOP = 8
EXP_NODE = 8
CAP = 2
LANES = 128
SUBLANES = 8
VMEM_BYTES = 56 << 20
FLOPS_CUT = 2 * 10**10
FLOPS_PART = 3 * 10**10

COLS = (((1,), (1,)), ((), ()))
ROWS = (((0,), (0,)), ((), ()))
PLAIN = (((1,), (0,)), ((), ()))


def dot(a, b, dims):
    return lax.dot_general(a, b, dims, preferred_element_type=jnp.float32)


def right(part, ring):
    return lax.ppermute(part, "block", [(i, (i + 1) % ring) for i in range(ring)])


def left(part, ring):
    return lax.ppermute(part, "block", [(i, (i - 1) % ring) for i in range(ring)])


def on_core(body, far_ins, near_ins, far_outs, near_outs, flops):
    n_in, n_near, n_out = len(far_ins), len(near_ins), len(far_outs)
    size = sum(v.size * v.dtype.itemsize for v in (*far_ins, *near_ins, *far_outs, *near_outs))

    def kernel(*refs):
        ends = [n_in, n_near, n_out, len(near_outs), n_in, n_out, 1, 1]
        groups, at = [], 0
        for count in ends:
            groups.append(refs[at : at + count])
            at += count
        source, near_in, target, near_out, held_in, held_out, (in_sem,), (out_sem,) = groups
        incoming = [
            pltpu.make_async_copy(src, held, in_sem.at[i])
            for i, (src, held) in enumerate(zip(source, held_in))
        ]
        outgoing = [
            pltpu.make_async_copy(held, dst, out_sem.at[i])
            for i, (held, dst) in enumerate(zip(held_out, target))
        ]
        for copy in incoming:
            copy.start()
        body(
            [(copy.wait, held) for copy, held in zip(incoming, held_in)],
            near_in,
            [(copy.start, held) for copy, held in zip(outgoing, held_out)],
            near_out,
        )
        for copy in outgoing:
            copy.wait()

    hbm, vmem = pl.BlockSpec(memory_space=pltpu.HBM), pl.BlockSpec(memory_space=pltpu.VMEM)
    return pl.pallas_call(
        kernel,
        out_shape=[*far_outs, *near_outs],
        in_specs=[hbm] * n_in + [vmem] * n_near,
        out_specs=[hbm] * n_out + [vmem] * len(near_outs),
        scratch_shapes=[
            *[pltpu.VMEM(v.shape, v.dtype) for v in (*far_ins, *far_outs)],
            pltpu.SemaphoreType.DMA((n_in,)),
            pltpu.SemaphoreType.DMA((n_out,)),
        ],
        compiler_params=pltpu.CompilerParams(vmem_limit_bytes=VMEM_BYTES),
        cost_estimate=pl.CostEstimate(flops=int(flops), bytes_accessed=size, transcendentals=0),
    )(*far_ins, *near_ins)


def cut(whole, side):
    rows, columns = whole.shape
    half = columns // 2

    def kernel(whole_ref, half_ref, held, sem):
        for src, dst in (
            (whole_ref.at[:, side * half : (side + 1) * half], held),
            (held, half_ref),
        ):
            copy = pltpu.make_async_copy(src, dst, sem)
            copy.start()
            copy.wait()

    hbm = pl.BlockSpec(memory_space=pltpu.HBM)
    return pl.pallas_call(
        kernel,
        out_shape=jax.ShapeDtypeStruct((rows, half), whole.dtype),
        in_specs=[hbm],
        out_specs=hbm,
        scratch_shapes=[pltpu.VMEM((rows, half), whole.dtype), pltpu.SemaphoreType.DMA],
        compiler_params=pltpu.CompilerParams(vmem_limit_bytes=VMEM_BYTES),
        cost_estimate=pl.CostEstimate(flops=FLOPS_CUT, bytes_accessed=0, transcendentals=0),
    )(whole)


def halves(refs, rows):
    if len(refs) == 2:
        return [ref[rows] for ref in refs]
    half = refs[0].shape[1] // 2
    return [refs[0][rows, :half], refs[0][rows, half:]]


def split_parts(parts, items):
    out, at = [], 0
    for part in parts:
        out.append(items[at : at + part])
        at += part
    return out


def block_grads(width, units, rows_ref, weights, emits):
    half = width // 2
    gates, downs = slice(0, 2 * units), slice(2 * units, 3 * units)
    x = [rows_ref[:, :half], rows_ref[:, half:width]]
    dy = [rows_ref[:, width : width + half], rows_ref[:, width + half :]]
    pre = sum(dot(w, v, COLS) for w, v in zip(halves(weights, gates), x))
    d_act = sum(dot(w, v, COLS) for w, v in zip(halves(weights, downs), dy))
    pre_gate, pre_up = pre[:units], pre[units:]
    logistic = 1.0 / (1.0 + jnp.exp(-pre_gate))
    act = (pre_gate * logistic * pre_up).astype(jnp.bfloat16)
    d_s = jnp.sum(act.astype(jnp.float32) * d_act, axis=0, keepdims=True)
    d_gate = d_act * pre_up * logistic * (1.0 + pre_gate * (1.0 - logistic))
    d_up = d_act * pre_gate * logistic
    d_pre = jnp.concatenate([d_gate, d_up], axis=0)
    d_pre_low = d_pre.astype(jnp.bfloat16)
    for i, (send, grad) in enumerate(emits):
        grad[gates] = dot(d_pre_low, x[i], PLAIN).astype(grad.dtype)
        grad[downs] = dot(act, dy[i], PLAIN).astype(grad.dtype)
        send()
    return d_pre.T.astype(jnp.bfloat16), d_s


def blocks_body(width, units, parts, fetches, near_in, emits, near_out):
    (wait_rows, rows_ref), weights = fetches[0], split_parts(parts, fetches[1:])
    count = len(parts)
    wait_rows()
    total = sum(ref[:1] for ref in near_in)
    for b in range(count):
        for wait, _ in weights[b]:
            wait()
        refs = [ref for _, ref in weights[b]]
        out = emits[2 * b : 2 * b + 2]
        d_pre, d_s = block_grads(width, units, rows_ref, refs, out)
        near_out[b][...] = d_pre
        total = total + d_s
    near_out[count][...] = jnp.broadcast_to(total, near_out[count].shape)


def own_body(width, units, parts, fetches, near_in, emits, near_out):
    (wait_rows, rows_ref), weights = fetches[0], split_parts(parts, fetches[1:])
    count, half = len(parts), width // 2
    wait_rows()
    for wait, _ in weights[0]:
        wait()
    refs = [[ref for _, ref in pairs] for pairs in weights]
    d_pre, d_s = block_grads(width, units, rows_ref, refs[0], emits[:2])
    d_pre = [d_pre] + [ref[...] for ref in near_in[: count - 1]]
    d_s = d_s + near_in[count - 1][:1]
    for pairs in weights[1:]:
        for wait, _ in pairs:
            wait()
    send, out_ref = emits[2]
    gates = slice(0, 2 * units)
    for i in range(2):
        total = sum(dot(d_pre[b], halves(refs[b], gates)[i], PLAIN) for b in range(count))
        out_ref[:, i * half : (i + 1) * half] = total.astype(jnp.bfloat16)
    scores = jnp.broadcast_to(d_s, (LANES, d_s.shape[1])).T
    out_ref[:, width:] = scores.astype(jnp.bfloat16)
    send()


def add_body(fetches, near_in, emits, near_out):
    for i, (send, out) in enumerate(emits):
        (wait_a, a), (wait_b, b) = fetches[2 * i : 2 * i + 2]
        wait_a()
        wait_b()
        out[...] = (a[...].astype(jnp.float32) + b[...].astype(jnp.float32)).astype(out.dtype)
        send()


def added(*pairs, flops=0):
    outs = [jax.ShapeDtypeStruct(a.shape, a.dtype) for a, _ in pairs]
    return on_core(add_body, [v for pair in pairs for v in pair], [], outs, [], flops)


def total_body(units, fetches, near_in, emits, near_out):
    half = fetches[0][1].shape[1]
    for i in range(2):
        pair = fetches[2 * i : 2 * i + 2]
        for wait, _ in pair:
            wait()
        for j, (send, out) in enumerate(emits):
            rows = slice(j * units, (j + 1) * units)
            out[:, i * half : (i + 1) * half] = sum(
                ref[rows].astype(jnp.float32) for _, ref in pair
            ).astype(jnp.bfloat16)
            if i == 1:
                send()


def on_device(tokens, grad_out, expert_ids, scores, gate_weight, up_weight, down_weight):
    ring = lax.axis_size("block")
    expert_count = lax.axis_size("node") * lax.axis_size("expert")
    tok_count, width = tokens.shape
    units = gate_weight.shape[2]
    half = width // 2
    slot_count = expert_count * CAP
    bf16, f32 = jnp.bfloat16, jnp.float32
    shape = jax.ShapeDtypeStruct

    own = jnp.concatenate([gate_weight[0, 0], up_weight[0, 0], down_weight[0, 0]], axis=0)
    before = right(own, ring)
    after = left(own, ring)
    far_a = right(cut(before, 0), ring)
    far_b = left(cut(after, 1), ring)

    flat_ids = expert_ids.reshape(-1)
    expert_iota = jnp.arange(expert_count, dtype=jnp.int32)
    matches = (flat_ids[:, None] == expert_iota[None, :]).astype(jnp.int32)
    rank_within = jnp.sum((jnp.cumsum(matches, axis=0) - matches) * matches, axis=1)
    slot_index = flat_ids * CAP + rank_within
    placed = jnp.arange(slot_count, dtype=jnp.int32)[:, None] == slot_index[None, :]
    token_map = placed.reshape(slot_count, tok_count, TOP).sum(axis=2).astype(bf16)
    slot_s = jnp.sum(jnp.where(placed, scores.reshape(-1)[None, :].astype(f32), 0.0), axis=1)
    rows = dot(token_map, jnp.concatenate([tokens, grad_out], axis=1), PLAIN)
    by_slot = jnp.where(jnp.arange(2 * width)[None, :] < width, 1.0, slot_s[:, None])
    outgoing = (rows * by_slot).astype(bf16)
    rows = lax.all_to_all(
        outgoing.reshape(expert_count, CAP, 2 * width), ("node", "expert"), 0, 0, tiled=True
    ).reshape(slot_count, 2 * width)
    half_grad = shape((3 * units, half), bf16)
    near = [shape((slot_count, 2 * units), bf16), shape((SUBLANES, slot_count), f32)]

    def blocks(weights, so_far):
        count = len(weights)
        results = on_core(
            functools.partial(blocks_body, width, units, [len(w) for w in weights]),
            [rows, *[w for ws in weights for w in ws]],
            so_far,
            [half_grad] * (2 * count),
            [near[0]] * count + [near[1]],
            count * 12 * slot_count * units * width,
        )
        return results[: 2 * count], results[2 * count : 3 * count], results[3 * count :]

    (far_grad_a, far_grad_b), far_pre, far_s = blocks([(far_a, far_b)], [])
    passing_a = right(far_grad_a, ring)
    passing_b = left(far_grad_b, ring)
    (nxt_a, nxt_b, prev_a, prev_b), near_pre, near_s = blocks([(after,), (before,)], far_s)
    left_b = right(nxt_b, ring)
    right_a = left(prev_a, ring)
    left_a = right(added((nxt_a, passing_a))[0], ring)
    right_b = left(added((prev_b, passing_b))[0], ring)
    mine_a, mine_b, returning = on_core(
        functools.partial(own_body, width, units, [1, 2, 1, 1]),
        [rows, own, far_a, far_b, after, before],
        [*far_pre, *near_pre, *near_s],
        [half_grad, half_grad, shape((slot_count, width + LANES), bf16)],
        [],
        28 * slot_count * units * width,
    )
    part_a, part_b = added((mine_a, right_a), (mine_b, left_b), flops=FLOPS_PART)
    d_gate, d_up, d_down = on_core(
        functools.partial(total_body, units),
        [part_a, left_a, part_b, right_b],
        [],
        [shape((units, width), bf16)] * 3,
        [],
        0,
    )

    home = lax.all_to_all(
        returning.reshape(expert_count, CAP, width + LANES), ("node", "expert"), 0, 0, tiled=True
    ).reshape(slot_count, width + LANES)
    d_tokens = dot(token_map, home[:, :width], ROWS).astype(bf16)
    scaled_sums = jnp.sum(jnp.where(placed, home[:, width].astype(f32)[:, None], 0.0), axis=0)
    d_scores = (scaled_sums.reshape(tok_count, TOP) / scores.astype(f32)).astype(bf16)
    return (d_tokens, d_scores, d_gate[None, None], d_up[None, None], d_down[None, None])


def solution(mesh):
    node_count, local_count = mesh.devices.shape
    mesh = Mesh(
        mesh.devices.reshape(node_count, EXP_NODE, local_count // EXP_NODE),
        ("node", "expert", "block"),
    )
    by_token = P(("node", "expert", "block"), None)
    by_block = P("node", ("expert", "block"), None, None)
    return jax.shard_map(
        on_device,
        mesh=mesh,
        in_specs=(by_token,) * 4 + (by_block,) * 3,
        out_specs=(by_token,) * 2 + (by_block,) * 3,
        check_vma=False,
    )
```

```python
import functools

import jax
import jax.numpy as jnp
from jax import lax
from jax.experimental import pallas as pl
from jax.experimental.pallas import tpu as pltpu
from jax.sharding import Mesh
from jax.sharding import PartitionSpec as P

TOP = 8
EXP_NODE = 8
CAP = 2
LANES = 128
SUBLANES = 8
PIECES = 4
VMEM_BYTES = 58 << 20
FLOPS_CUT = 2 * 10**10
FLOPS_PART = 3 * 10**10

COLS = (((1,), (1,)), ((), ()))
ROWS = (((0,), (0,)), ((), ()))
PLAIN = (((1,), (0,)), ((), ()))


def dot(a, b, dims):
    return lax.dot_general(a, b, dims, preferred_element_type=jnp.float32)


def right(part, ring):
    return lax.ppermute(part, "block", [(i, (i + 1) % ring) for i in range(ring)])


def left(part, ring):
    return lax.ppermute(part, "block", [(i, (i - 1) % ring) for i in range(ring)])


def pieces(src, dst, sems):
    rows = src.shape[0] // PIECES
    spans = [pl.ds(i * rows, rows) for i in range(PIECES)]
    return [
        pltpu.make_async_copy(src.at[span], dst.at[span], sems.at[i])
        for i, span in enumerate(spans)
    ]


def each(copies, what):
    for copy in copies:
        getattr(copy, what)()


def on_core(body, far_ins, near_ins, far_outs, near_outs, flops):
    n_in, n_near, n_out = len(far_ins), len(near_ins), len(far_outs)
    size = sum(v.size * v.dtype.itemsize for v in (*far_ins, *near_ins, *far_outs, *near_outs))

    def kernel(*refs):
        ends = [n_in, n_near, n_out, len(near_outs), n_in, n_out, 1, 1]
        groups, at = [], 0
        for count in ends:
            groups.append(refs[at : at + count])
            at += count
        source, near_in, target, near_out, held_in, held_out, (in_sem,), (out_sem,) = groups
        incoming = [pieces(src, held, in_sem.at[i]) for i, (src, held) in enumerate(zip(source, held_in))]
        outgoing = [
            pieces(held, dst, out_sem.at[i]) for i, (held, dst) in enumerate(zip(held_out, target))
        ]
        for copies in incoming:
            each(copies, "start")
        body(
            [(functools.partial(each, c, "wait"), held) for c, held in zip(incoming, held_in)],
            near_in,
            [(functools.partial(each, c, "start"), held) for c, held in zip(outgoing, held_out)],
            near_out,
        )
        for copies in outgoing:
            each(copies, "wait")

    hbm, vmem = pl.BlockSpec(memory_space=pltpu.HBM), pl.BlockSpec(memory_space=pltpu.VMEM)
    return pl.pallas_call(
        kernel,
        out_shape=[*far_outs, *near_outs],
        in_specs=[hbm] * n_in + [vmem] * n_near,
        out_specs=[hbm] * n_out + [vmem] * len(near_outs),
        scratch_shapes=[
            *[pltpu.VMEM(v.shape, v.dtype) for v in (*far_ins, *far_outs)],
            pltpu.SemaphoreType.DMA((n_in, PIECES)),
            pltpu.SemaphoreType.DMA((n_out, PIECES)),
        ],
        compiler_params=pltpu.CompilerParams(vmem_limit_bytes=VMEM_BYTES),
        cost_estimate=pl.CostEstimate(flops=int(flops), bytes_accessed=size, transcendentals=0),
    )(*far_ins, *near_ins)


def hold(part):
    hbm = pl.BlockSpec(memory_space=pltpu.HBM)
    return pl.pallas_call(
        lambda part_ref, same_ref: None,
        out_shape=jax.ShapeDtypeStruct(part.shape, part.dtype),
        in_specs=[hbm],
        out_specs=hbm,
        input_output_aliases={0: 0},
        compiler_params=pltpu.CompilerParams(vmem_limit_bytes=1 << 20),
        cost_estimate=pl.CostEstimate(flops=FLOPS_CUT, bytes_accessed=0, transcendentals=0),
    )(part)


def halves(refs, rows):
    if len(refs) == 2:
        return [ref[rows] for ref in refs]
    half = refs[0].shape[1] // 2
    return [refs[0][rows, :half], refs[0][rows, half:]]


def split_parts(parts, items):
    out, at = [], 0
    for part in parts:
        out.append(items[at : at + part])
        at += part
    return out


def block_grads(width, units, rows_ref, weights, emits):
    half = width // 2
    gates, downs = slice(0, 2 * units), slice(2 * units, 3 * units)
    x = [rows_ref[:, :half], rows_ref[:, half:width]]
    dy = [rows_ref[:, width : width + half], rows_ref[:, width + half :]]
    pre = sum(dot(w, v, COLS) for w, v in zip(halves(weights, gates), x))
    d_act = sum(dot(w, v, COLS) for w, v in zip(halves(weights, downs), dy))
    pre_gate, pre_up = pre[:units], pre[units:]
    logistic = 1.0 / (1.0 + jnp.exp(-pre_gate))
    act = (pre_gate * logistic * pre_up).astype(jnp.bfloat16)
    d_s = jnp.sum(act.astype(jnp.float32) * d_act, axis=0, keepdims=True)
    d_gate = d_act * pre_up * logistic * (1.0 + pre_gate * (1.0 - logistic))
    d_up = d_act * pre_gate * logistic
    d_pre = jnp.concatenate([d_gate, d_up], axis=0)
    d_pre_low = d_pre.astype(jnp.bfloat16)
    for i, (send, grad) in enumerate(emits):
        grad[gates] = dot(d_pre_low, x[i], PLAIN).astype(grad.dtype)
        grad[downs] = dot(act, dy[i], PLAIN).astype(grad.dtype)
        send()
    return d_pre.T.astype(jnp.bfloat16), d_s


def blocks_body(width, units, parts, fetches, near_in, emits, near_out):
    (wait_rows, rows_ref), weights = fetches[0], split_parts(parts, fetches[1:])
    count = len(parts)
    wait_rows()
    if len(rows_ref.shape) == 3:
        send_rows, flat_ref = emits[2 * count]
        flat_ref[...] = rows_ref[...].reshape(flat_ref.shape)
        send_rows()
        rows_ref = flat_ref
    total = sum(ref[:1] for ref in near_in)
    for b in range(count):
        for wait, _ in weights[b]:
            wait()
        refs = [ref for _, ref in weights[b]]
        out = emits[2 * b : 2 * b + 2]
        d_pre, d_s = block_grads(width, units, rows_ref, refs, out)
        near_out[b][...] = d_pre
        total = total + d_s
    near_out[count][...] = jnp.broadcast_to(total, near_out[count].shape)


def own_body(width, units, parts, fetches, near_in, emits, near_out):
    (wait_rows, rows_ref), weights = fetches[0], split_parts(parts, fetches[1:])
    count, half = len(parts), width // 2
    wait_rows()
    for wait, _ in weights[0]:
        wait()
    refs = [[ref for _, ref in pairs] for pairs in weights]
    d_pre, d_s = block_grads(width, units, rows_ref, refs[0], emits[:2])
    d_pre = [d_pre] + [ref[...] for ref in near_in[: count - 1]]
    d_s = d_s + near_in[count - 1][:1]
    for pairs in weights[1:]:
        for wait, _ in pairs:
            wait()
    send, out_ref = emits[2]
    gates = slice(0, 2 * units)
    for i in range(2):
        total = sum(dot(d_pre[b], halves(refs[b], gates)[i], PLAIN) for b in range(count))
        total = total.astype(jnp.bfloat16).reshape((*out_ref.shape[:2], half))
        out_ref[:, :, i * half : (i + 1) * half] = total
    scores = jnp.broadcast_to(d_s, (LANES, d_s.shape[1])).T.astype(jnp.bfloat16)
    out_ref[:, :, width:] = scores.reshape((*out_ref.shape[:2], LANES))
    send()


def add_body(fetches, near_in, emits, near_out):
    for i, (send, out) in enumerate(emits):
        (wait_a, a), (wait_b, b) = fetches[2 * i : 2 * i + 2]
        wait_a()
        wait_b()
        out[...] = (a[...].astype(jnp.float32) + b[...].astype(jnp.float32)).astype(out.dtype)
        send()


def added(*pairs, flops=0):
    outs = [jax.ShapeDtypeStruct(a.shape, a.dtype) for a, _ in pairs]
    return on_core(add_body, [v for pair in pairs for v in pair], [], outs, [], flops)


def total_body(units, fetches, near_in, emits, near_out):
    half = fetches[0][1].shape[1]
    for i in range(2):
        pair = fetches[2 * i : 2 * i + 2]
        for wait, _ in pair:
            wait()
        for j, (send, out) in enumerate(emits):
            rows = slice(j * units, (j + 1) * units)
            out[:, i * half : (i + 1) * half] = sum(
                ref[rows].astype(jnp.float32) for _, ref in pair
            ).astype(jnp.bfloat16)
            if i == 1:
                send()


def matched(ids, expert_slots, k):
    return ids[k : k + 1] == expert_slots


def dispatch_body(ids_ref, scores_ref, tokens_ref, grad_ref, rows_ref, map_ref):
    slot_count, width = map_ref.shape[0], tokens_ref.shape[1]
    tok_count = tokens_ref.shape[0]
    shape = (slot_count, tok_count)
    slots = lax.broadcasted_iota(jnp.int32, shape, 0)
    ids, scores = ids_ref[...], scores_ref[...].astype(jnp.float32)
    named, weight = jnp.zeros(shape, jnp.float32), jnp.zeros(shape, jnp.float32)
    for k in range(TOP):
        hit = matched(ids, slots // CAP, k)
        named = jnp.where(hit, 1.0, named)
        weight = jnp.where(hit, scores[k : k + 1], weight)
    square = (tok_count, tok_count)
    earlier = lax.broadcasted_iota(jnp.int32, square, 0) < lax.broadcasted_iota(jnp.int32, square, 1)
    rank = dot(named.astype(jnp.bfloat16), earlier.astype(jnp.bfloat16), PLAIN)
    placed = jnp.where(rank == (slots % CAP).astype(jnp.float32), named, 0.0)
    slot_s = jnp.sum(placed * weight, axis=1, keepdims=True)
    token_map = placed.astype(jnp.bfloat16)
    map_ref[...] = token_map
    x = dot(token_map, tokens_ref[...], PLAIN).astype(jnp.bfloat16)
    rows_ref[:, :, :width] = x.reshape(slot_count // CAP, CAP, width)
    scaled = slot_s * dot(token_map, grad_ref[...], PLAIN)
    rows_ref[:, :, width:] = scaled.astype(jnp.bfloat16).reshape(slot_count // CAP, CAP, width)


def home_body(home_ref, ids_ref, scores_ref, map_ref, tokens_ref, out_scores_ref):
    width = tokens_ref.shape[1]
    token_map = map_ref[...]
    home = home_ref[...].reshape(token_map.shape[0], width + LANES)
    tokens_ref[...] = dot(token_map, home[:, :width], ROWS).astype(jnp.bfloat16)
    slots = lax.broadcasted_iota(jnp.int32, token_map.shape, 0)
    ids, scores = ids_ref[...], scores_ref[...].astype(jnp.float32)
    sums = token_map.astype(jnp.float32) * home[:, width : width + 1].astype(jnp.float32)
    for k in range(TOP):
        own = jnp.where(matched(ids, slots // CAP, k), sums, 0.0)
        total = jnp.sum(own, axis=0, keepdims=True) / scores[k : k + 1]
        out_scores_ref[k : k + 1] = total


def simple_call(body, outs, *operands):
    vmem = pl.BlockSpec(memory_space=pltpu.VMEM)
    size = sum(v.size * v.dtype.itemsize for v in (*operands, *outs))
    return pl.pallas_call(
        body,
        out_shape=outs,
        in_specs=[vmem] * len(operands),
        out_specs=[vmem] * len(outs),
        compiler_params=pltpu.CompilerParams(vmem_limit_bytes=16 << 20),
        cost_estimate=pl.CostEstimate(flops=0, bytes_accessed=size, transcendentals=0),
    )(*operands)


def on_device(tokens, grad_out, expert_ids, scores, gate_weight, up_weight, down_weight):
    ring = lax.axis_size("block")
    expert_count = lax.axis_size("node") * lax.axis_size("expert")
    tok_count, width = tokens.shape
    units = gate_weight.shape[2]
    half = width // 2
    slot_count = expert_count * CAP
    bf16, f32 = jnp.bfloat16, jnp.float32
    shape = jax.ShapeDtypeStruct

    matrices = [gate_weight[0, 0], up_weight[0, 0], down_weight[0, 0]]
    own_a = jnp.concatenate([w[:, :half] for w in matrices], axis=0)
    own_b = jnp.concatenate([w[:, half:] for w in matrices], axis=0)
    before_a, after_b = hold(right(own_a, ring)), hold(left(own_b, ring))
    before = (before_a, right(own_b, ring))
    after = (left(own_a, ring), after_b)
    far_a, far_b = right(before_a, ring), left(after_b, ring)

    ids_t, scores_t = expert_ids.T, scores.T
    outgoing, token_map = simple_call(
        dispatch_body,
        [shape((expert_count, CAP, 2 * width), bf16), shape((slot_count, tok_count), bf16)],
        ids_t,
        scores_t,
        tokens,
        grad_out,
    )
    rows = lax.all_to_all(
        outgoing, ("node", "expert"), 0, 0, tiled=True
    )
    half_grad = shape((3 * units, half), bf16)
    near = [shape((slot_count, 2 * units), bf16), shape((SUBLANES, slot_count), f32)]

    def blocks(weights, so_far, rows, extra=()):
        count = len(weights)
        results = on_core(
            functools.partial(blocks_body, width, units, [len(w) for w in weights]),
            [rows, *[w for ws in weights for w in ws]],
            so_far,
            [half_grad] * (2 * count) + list(extra),
            [near[0]] * count + [near[1]],
            count * 12 * slot_count * units * width,
        )
        sent = 2 * count + len(extra)
        return results[:sent], results[sent : sent + count], results[sent + count :]

    (far_grad_a, far_grad_b, flat_rows), far_pre, far_s = blocks(
        [(far_a, far_b)], [], rows, [shape((slot_count, 2 * width), bf16)]
    )
    passing_a = right(far_grad_a, ring)
    passing_b = left(far_grad_b, ring)
    (nxt_a, nxt_b, prev_a, prev_b), near_pre, near_s = blocks(
        [after, before], far_s, flat_rows
    )
    left_b = right(nxt_b, ring)
    right_a = left(prev_a, ring)
    left_a = right(added((nxt_a, passing_a))[0], ring)
    right_b = left(added((prev_b, passing_b))[0], ring)
    mine_a, mine_b, returning = on_core(
        functools.partial(own_body, width, units, [2, 2, 2, 2]),
        [flat_rows, own_a, own_b, far_a, far_b, *after, *before],
        [*far_pre, *near_pre, *near_s],
        [half_grad, half_grad, shape((expert_count, CAP, width + LANES), bf16)],
        [],
        28 * slot_count * units * width,
    )
    part_a, part_b = added((mine_a, right_a), (mine_b, left_b), flops=FLOPS_PART)
    d_gate, d_up, d_down = on_core(
        functools.partial(total_body, units),
        [part_a, left_a, part_b, right_b],
        [],
        [shape((units, width), bf16)] * 3,
        [],
        0,
    )

    home = lax.all_to_all(
        returning, ("node", "expert"), 0, 0, tiled=True
    )
    d_tokens, d_scores_t = simple_call(
        home_body,
        [shape((tok_count, width), bf16), shape((TOP, tok_count), f32)],
        home,
        ids_t,
        scores_t,
        token_map,
    )
    d_scores = d_scores_t.T.astype(bf16)
    return (d_tokens, d_scores, d_gate[None, None], d_up[None, None], d_down[None, None])


def solution(mesh):
    node_count, local_count = mesh.devices.shape
    mesh = Mesh(
        mesh.devices.reshape(node_count, EXP_NODE, local_count // EXP_NODE),
        ("node", "expert", "block"),
    )
    by_token = P(("node", "expert", "block"), None)
    by_block = P("node", ("expert", "block"), None, None)
    return jax.shard_map(
        on_device,
        mesh=mesh,
        in_specs=(by_token,) * 4 + (by_block,) * 3,
        out_specs=(by_token,) * 2 + (by_block,) * 3,
        check_vma=False,
    )
```

```python
import functools

import jax
import jax.numpy as jnp
from jax import lax
from jax.experimental import pallas as pl
from jax.experimental.pallas import tpu as pltpu
from jax.sharding import Mesh
from jax.sharding import PartitionSpec as P

TOP = 8
EXP_NODE = 8
CAP = 2
LANES = 128
SUBLANES = 8
PIECES = 4
VMEM_BYTES = 58 << 20
FLOPS_CUT = 2 * 10**10
FLOPS_PART = 3 * 10**10

COLS = (((1,), (1,)), ((), ()))
ROWS = (((0,), (0,)), ((), ()))
PLAIN = (((1,), (0,)), ((), ()))


def dot(a, b, dims):
    return lax.dot_general(a, b, dims, preferred_element_type=jnp.float32)


def right(part, ring):
    return lax.ppermute(part, "block", [(i, (i + 1) % ring) for i in range(ring)])


def left(part, ring):
    return lax.ppermute(part, "block", [(i, (i - 1) % ring) for i in range(ring)])


def pieces(src, dst, sems):
    rows = src.shape[0] // PIECES
    spans = [pl.ds(i * rows, rows) for i in range(PIECES)]
    return [
        pltpu.make_async_copy(src.at[span], dst.at[span], sems.at[i])
        for i, span in enumerate(spans)
    ]


def each(copies, what):
    for copy in copies:
        getattr(copy, what)()


def on_core(body, far_ins, near_ins, far_outs, near_outs, flops):
    n_in, n_near, n_out = len(far_ins), len(near_ins), len(far_outs)
    size = sum(v.size * v.dtype.itemsize for v in (*far_ins, *near_ins, *far_outs, *near_outs))

    def kernel(*refs):
        ends = [n_in, n_near, n_out, len(near_outs), n_in, n_out, 1, 1]
        groups, at = [], 0
        for count in ends:
            groups.append(refs[at : at + count])
            at += count
        source, near_in, target, near_out, held_in, held_out, (in_sem,), (out_sem,) = groups
        incoming = [pieces(src, held, in_sem.at[i]) for i, (src, held) in enumerate(zip(source, held_in))]
        outgoing = [
            pieces(held, dst, out_sem.at[i]) for i, (held, dst) in enumerate(zip(held_out, target))
        ]
        for copies in incoming:
            each(copies, "start")
        body(
            [(functools.partial(each, c, "wait"), held) for c, held in zip(incoming, held_in)],
            near_in,
            [(functools.partial(each, c, "start"), held) for c, held in zip(outgoing, held_out)],
            near_out,
        )
        for copies in outgoing:
            each(copies, "wait")

    hbm, vmem = pl.BlockSpec(memory_space=pltpu.HBM), pl.BlockSpec(memory_space=pltpu.VMEM)
    return pl.pallas_call(
        kernel,
        out_shape=[*far_outs, *near_outs],
        in_specs=[hbm] * n_in + [vmem] * n_near,
        out_specs=[hbm] * n_out + [vmem] * len(near_outs),
        scratch_shapes=[
            *[pltpu.VMEM(v.shape, v.dtype) for v in (*far_ins, *far_outs)],
            pltpu.SemaphoreType.DMA((n_in, PIECES)),
            pltpu.SemaphoreType.DMA((n_out, PIECES)),
        ],
        compiler_params=pltpu.CompilerParams(vmem_limit_bytes=VMEM_BYTES),
        cost_estimate=pl.CostEstimate(flops=int(flops), bytes_accessed=size, transcendentals=0),
    )(*far_ins, *near_ins)


def hold(part):
    hbm = pl.BlockSpec(memory_space=pltpu.HBM)
    return pl.pallas_call(
        lambda part_ref, same_ref: None,
        out_shape=jax.ShapeDtypeStruct(part.shape, part.dtype),
        in_specs=[hbm],
        out_specs=hbm,
        input_output_aliases={0: 0},
        compiler_params=pltpu.CompilerParams(vmem_limit_bytes=1 << 20),
        cost_estimate=pl.CostEstimate(flops=FLOPS_CUT, bytes_accessed=0, transcendentals=0),
    )(part)


def halves(refs, rows):
    if len(refs) == 2:
        return [ref[rows] for ref in refs]
    half = refs[0].shape[1] // 2
    return [refs[0][rows, :half], refs[0][rows, half:]]


def split_parts(parts, items):
    out, at = [], 0
    for part in parts:
        out.append(items[at : at + part])
        at += part
    return out


def block_grads(width, units, rows_ref, weights, emits):
    half = width // 2
    gates, downs = slice(0, 2 * units), slice(2 * units, 3 * units)
    x = [rows_ref[:, :half], rows_ref[:, half:width]]
    dy = [rows_ref[:, width : width + half], rows_ref[:, width + half :]]
    pre = sum(dot(w, v, COLS) for w, v in zip(halves(weights, gates), x))
    d_act = sum(dot(w, v, COLS) for w, v in zip(halves(weights, downs), dy))
    pre_gate, pre_up = pre[:units], pre[units:]
    logistic = 1.0 / (1.0 + jnp.exp(-pre_gate))
    act = (pre_gate * logistic * pre_up).astype(jnp.bfloat16)
    d_s = jnp.sum(act.astype(jnp.float32) * d_act, axis=0, keepdims=True)
    d_gate = d_act * pre_up * logistic * (1.0 + pre_gate * (1.0 - logistic))
    d_up = d_act * pre_gate * logistic
    d_pre = jnp.concatenate([d_gate, d_up], axis=0)
    d_pre_low = d_pre.astype(jnp.bfloat16)
    for i, (send, grad) in enumerate(emits):
        grad[gates] = dot(d_pre_low, x[i], PLAIN).astype(grad.dtype)
        grad[downs] = dot(act, dy[i], PLAIN).astype(grad.dtype)
        send()
    return d_pre.T.astype(jnp.bfloat16), d_s


def far_body(width, units, fetches, near_in, emits, near_out):
    (wait_rows, rows_ref), weights = fetches[0], fetches[1:]
    wait_rows()
    send_rows, flat_ref = emits[2]
    flat_ref[...] = rows_ref[...].reshape(flat_ref.shape)
    send_rows()
    for wait, _ in weights:
        wait()
    refs = [ref for _, ref in weights]
    d_pre, d_s = block_grads(width, units, flat_ref, refs, emits[:2])
    near_out[0][...] = d_pre
    near_out[1][...] = jnp.broadcast_to(d_s, near_out[1].shape)


def rest_body(width, units, parts, fetches, near_in, emits, near_out):
    (wait_rows, rows_ref), weights = fetches[0], split_parts(parts, fetches[1:])
    count, half = len(parts), width // 2
    refs = [[ref for _, ref in pairs] for pairs in weights]
    wait_rows()
    d_pre, d_s = [near_in[0][...]], near_in[1][:1]
    for b in range(count):
        for wait, _ in weights[b]:
            wait()
        if b > 0:
            grads = emits[2 * (b - 1) : 2 * b]
            terms = block_grads(width, units, rows_ref, refs[b], grads)
            d_pre.append(terms[0])
            d_s = d_s + terms[1]
    send, out_ref = emits[-1]
    gates = slice(0, 2 * units)
    for i in range(2):
        total = sum(dot(d_pre[b], halves(refs[b], gates)[i], PLAIN) for b in range(count))
        total = total.astype(jnp.bfloat16).reshape((*out_ref.shape[:2], half))
        out_ref[:, :, i * half : (i + 1) * half] = total
    scores = jnp.broadcast_to(d_s, (LANES, d_s.shape[1])).T.astype(jnp.bfloat16)
    out_ref[:, :, width:] = scores.reshape((*out_ref.shape[:2], LANES))
    send()


def add_body(fetches, near_in, emits, near_out):
    for i, (send, out) in enumerate(emits):
        (wait_a, a), (wait_b, b) = fetches[2 * i : 2 * i + 2]
        wait_a()
        wait_b()
        out[...] = (a[...].astype(jnp.float32) + b[...].astype(jnp.float32)).astype(out.dtype)
        send()


def added(*pairs, flops=0):
    outs = [jax.ShapeDtypeStruct(a.shape, a.dtype) for a, _ in pairs]
    return on_core(add_body, [v for pair in pairs for v in pair], [], outs, [], flops)


def total_body(units, fetches, near_in, emits, near_out):
    half = fetches[0][1].shape[1]
    for i in range(2):
        pair = fetches[2 * i : 2 * i + 2]
        for wait, _ in pair:
            wait()
        for j, (send, out) in enumerate(emits):
            rows = slice(j * units, (j + 1) * units)
            out[:, i * half : (i + 1) * half] = sum(
                ref[rows].astype(jnp.float32) for _, ref in pair
            ).astype(jnp.bfloat16)
            if i == 1:
                send()


def matched(ids, expert_slots, k):
    return ids[k : k + 1] == expert_slots


def dispatch_body(ids_ref, scores_ref, tokens_ref, grad_ref, rows_ref, map_ref):
    slot_count, width = map_ref.shape[0], tokens_ref.shape[1]
    tok_count = tokens_ref.shape[0]
    shape = (slot_count, tok_count)
    slots = lax.broadcasted_iota(jnp.int32, shape, 0)
    ids, scores = ids_ref[...], scores_ref[...].astype(jnp.float32)
    named, weight = jnp.zeros(shape, jnp.float32), jnp.zeros(shape, jnp.float32)
    for k in range(TOP):
        hit = matched(ids, slots // CAP, k)
        named = jnp.where(hit, 1.0, named)
        weight = jnp.where(hit, scores[k : k + 1], weight)
    square = (tok_count, tok_count)
    earlier = lax.broadcasted_iota(jnp.int32, square, 0) < lax.broadcasted_iota(jnp.int32, square, 1)
    rank = dot(named.astype(jnp.bfloat16), earlier.astype(jnp.bfloat16), PLAIN)
    placed = jnp.where(rank == (slots % CAP).astype(jnp.float32), named, 0.0)
    slot_s = jnp.sum(placed * weight, axis=1, keepdims=True)
    token_map = placed.astype(jnp.bfloat16)
    map_ref[...] = token_map
    x = dot(token_map, tokens_ref[...], PLAIN).astype(jnp.bfloat16)
    rows_ref[:, :, :width] = x.reshape(slot_count // CAP, CAP, width)
    scaled = slot_s * dot(token_map, grad_ref[...], PLAIN)
    rows_ref[:, :, width:] = scaled.astype(jnp.bfloat16).reshape(slot_count // CAP, CAP, width)


def home_body(home_ref, ids_ref, scores_ref, map_ref, tokens_ref, out_scores_ref):
    width = tokens_ref.shape[1]
    token_map = map_ref[...]
    home = home_ref[...].reshape(token_map.shape[0], width + LANES)
    tokens_ref[...] = dot(token_map, home[:, :width], ROWS).astype(jnp.bfloat16)
    slots = lax.broadcasted_iota(jnp.int32, token_map.shape, 0)
    ids, scores = ids_ref[...], scores_ref[...].astype(jnp.float32)
    sums = token_map.astype(jnp.float32) * home[:, width : width + 1].astype(jnp.float32)
    for k in range(TOP):
        own = jnp.where(matched(ids, slots // CAP, k), sums, 0.0)
        total = jnp.sum(own, axis=0, keepdims=True) / scores[k : k + 1]
        out_scores_ref[k : k + 1] = total


def simple_call(body, outs, *operands):
    vmem = pl.BlockSpec(memory_space=pltpu.VMEM)
    size = sum(v.size * v.dtype.itemsize for v in (*operands, *outs))
    return pl.pallas_call(
        body,
        out_shape=outs,
        in_specs=[vmem] * len(operands),
        out_specs=[vmem] * len(outs),
        compiler_params=pltpu.CompilerParams(vmem_limit_bytes=16 << 20),
        cost_estimate=pl.CostEstimate(flops=0, bytes_accessed=size, transcendentals=0),
    )(*operands)


def on_device(tokens, grad_out, expert_ids, scores, gate_weight, up_weight, down_weight):
    ring = lax.axis_size("block")
    expert_count = lax.axis_size("node") * lax.axis_size("expert")
    tok_count, width = tokens.shape
    units = gate_weight.shape[2]
    half = width // 2
    slot_count = expert_count * CAP
    bf16, f32 = jnp.bfloat16, jnp.float32
    shape = jax.ShapeDtypeStruct

    matrices = [gate_weight[0, 0], up_weight[0, 0], down_weight[0, 0]]
    own_a = jnp.concatenate([w[:, :half] for w in matrices], axis=0)
    own_b = jnp.concatenate([w[:, half:] for w in matrices], axis=0)
    before_a, after_b = hold(right(own_a, ring)), hold(left(own_b, ring))
    before = (before_a, right(own_b, ring))
    after = (left(own_a, ring), after_b)
    far_a, far_b = right(before_a, ring), left(after_b, ring)

    ids_t, scores_t = expert_ids.T, scores.T
    outgoing, token_map = simple_call(
        dispatch_body,
        [shape((expert_count, CAP, 2 * width), bf16), shape((slot_count, tok_count), bf16)],
        ids_t,
        scores_t,
        tokens,
        grad_out,
    )
    rows = lax.all_to_all(
        outgoing, ("node", "expert"), 0, 0, tiled=True
    )
    half_grad = shape((3 * units, half), bf16)
    block_flops = 12 * slot_count * units * width

    far_grad_a, far_grad_b, flat_rows, far_pre, far_s = on_core(
        functools.partial(far_body, width, units),
        [rows, far_a, far_b],
        [],
        [half_grad, half_grad, shape((slot_count, 2 * width), bf16)],
        [shape((slot_count, 2 * units), bf16), shape((SUBLANES, slot_count), f32)],
        block_flops,
    )
    passing_a = right(far_grad_a, ring)
    passing_b = left(far_grad_b, ring)
    nxt_a, nxt_b, prev_a, prev_b, mine_a, mine_b, returning = on_core(
        functools.partial(rest_body, width, units, [2] * ring),
        [flat_rows, far_a, far_b, *after, *before, own_a, own_b],
        [far_pre, far_s],
        [half_grad] * 6 + [shape((expert_count, CAP, width + LANES), bf16)],
        [],
        4 * block_flops,
    )
    left_b = right(nxt_b, ring)
    right_a = left(prev_a, ring)
    left_a = right((nxt_a.astype(f32) + passing_a.astype(f32)).astype(bf16), ring)
    right_b = left((prev_b.astype(f32) + passing_b.astype(f32)).astype(bf16), ring)
    part_a, part_b = added((mine_a, right_a), (mine_b, left_b), flops=FLOPS_PART)
    d_gate, d_up, d_down = on_core(
        functools.partial(total_body, units),
        [part_a, left_a, part_b, right_b],
        [],
        [shape((units, width), bf16)] * 3,
        [],
        0,
    )

    home = lax.all_to_all(
        returning, ("node", "expert"), 0, 0, tiled=True
    )
    d_tokens, d_scores_t = simple_call(
        home_body,
        [shape((tok_count, width), bf16), shape((TOP, tok_count), f32)],
        home,
        ids_t,
        scores_t,
        token_map,
    )
    d_scores = d_scores_t.T.astype(bf16)
    return (d_tokens, d_scores, d_gate[None, None], d_up[None, None], d_down[None, None])


def solution(mesh):
    node_count, local_count = mesh.devices.shape
    mesh = Mesh(
        mesh.devices.reshape(node_count, EXP_NODE, local_count // EXP_NODE),
        ("node", "expert", "block"),
    )
    by_token = P(("node", "expert", "block"), None)
    by_block = P("node", ("expert", "block"), None, None)
    return jax.shard_map(
        on_device,
        mesh=mesh,
        in_specs=(by_token,) * 4 + (by_block,) * 3,
        out_specs=(by_token,) * 2 + (by_block,) * 3,
        check_vma=False,
    )
```

```python
import functools

import jax
import jax.numpy as jnp
from jax import lax
from jax.experimental import pallas as pl
from jax.experimental.pallas import tpu as pltpu
from jax.sharding import Mesh
from jax.sharding import PartitionSpec as P

TOP = 8
EXP_NODE = 8
CAP = 2
LANES = 128
SUBLANES = 8
PIECES = 4
VMEM_BYTES = 58 << 20
FLOPS_CUT = 2 * 10**10
FLOPS_PART = 3 * 10**10

COLS = (((1,), (1,)), ((), ()))
ROWS = (((0,), (0,)), ((), ()))
PLAIN = (((1,), (0,)), ((), ()))


def dot(a, b, dims):
    return lax.dot_general(a, b, dims, preferred_element_type=jnp.float32)


def right(part, ring):
    return lax.ppermute(part, "block", [(i, (i + 1) % ring) for i in range(ring)])


def left(part, ring):
    return lax.ppermute(part, "block", [(i, (i - 1) % ring) for i in range(ring)])


def pieces(src, dst, sems):
    rows = src.shape[0] // PIECES
    spans = [pl.ds(i * rows, rows) for i in range(PIECES)]
    return [
        pltpu.make_async_copy(src.at[span], dst.at[span], sems.at[i])
        for i, span in enumerate(spans)
    ]


def each(copies, what):
    for copy in copies:
        getattr(copy, what)()


def on_core(body, far_ins, near_ins, far_outs, near_outs, flops):
    n_in, n_near, n_out = len(far_ins), len(near_ins), len(far_outs)
    size = sum(v.size * v.dtype.itemsize for v in (*far_ins, *near_ins, *far_outs, *near_outs))

    def kernel(*refs):
        ends = [n_in, n_near, n_out, len(near_outs), n_in, n_out, 1, 1]
        groups, at = [], 0
        for count in ends:
            groups.append(refs[at : at + count])
            at += count
        source, near_in, target, near_out, held_in, held_out, (in_sem,), (out_sem,) = groups
        incoming = [pieces(src, held, in_sem.at[i]) for i, (src, held) in enumerate(zip(source, held_in))]
        outgoing = [
            pieces(held, dst, out_sem.at[i]) for i, (held, dst) in enumerate(zip(held_out, target))
        ]
        for copies in incoming:
            each(copies, "start")
        body(
            [(functools.partial(each, c, "wait"), held) for c, held in zip(incoming, held_in)],
            near_in,
            [(functools.partial(each, c, "start"), held) for c, held in zip(outgoing, held_out)],
            near_out,
        )
        for copies in outgoing:
            each(copies, "wait")

    hbm, vmem = pl.BlockSpec(memory_space=pltpu.HBM), pl.BlockSpec(memory_space=pltpu.VMEM)
    return pl.pallas_call(
        kernel,
        out_shape=[*far_outs, *near_outs],
        in_specs=[hbm] * n_in + [vmem] * n_near,
        out_specs=[hbm] * n_out + [vmem] * len(near_outs),
        scratch_shapes=[
            *[pltpu.VMEM(v.shape, v.dtype) for v in (*far_ins, *far_outs)],
            pltpu.SemaphoreType.DMA((n_in, PIECES)),
            pltpu.SemaphoreType.DMA((n_out, PIECES)),
        ],
        compiler_params=pltpu.CompilerParams(vmem_limit_bytes=VMEM_BYTES),
        cost_estimate=pl.CostEstimate(flops=int(flops), bytes_accessed=size, transcendentals=0),
    )(*far_ins, *near_ins)


def hold(part):
    hbm = pl.BlockSpec(memory_space=pltpu.HBM)
    return pl.pallas_call(
        lambda part_ref, same_ref: None,
        out_shape=jax.ShapeDtypeStruct(part.shape, part.dtype),
        in_specs=[hbm],
        out_specs=hbm,
        input_output_aliases={0: 0},
        compiler_params=pltpu.CompilerParams(vmem_limit_bytes=1 << 20),
        cost_estimate=pl.CostEstimate(flops=FLOPS_CUT, bytes_accessed=0, transcendentals=0),
    )(part)


def halves(refs, rows):
    if len(refs) == 2:
        return [ref[rows] for ref in refs]
    half = refs[0].shape[1] // 2
    return [refs[0][rows, :half], refs[0][rows, half:]]


def split_parts(parts, items):
    out, at = [], 0
    for part in parts:
        out.append(items[at : at + part])
        at += part
    return out


def block_grads(width, units, rows_ref, weights, emits):
    half = width // 2
    gates, downs = slice(0, 2 * units), slice(2 * units, 3 * units)
    x = [rows_ref[:, :half], rows_ref[:, half:width]]
    dy = [rows_ref[:, width : width + half], rows_ref[:, width + half :]]
    pre = sum(dot(w, v, COLS) for w, v in zip(halves(weights, gates), x))
    d_act = sum(dot(w, v, COLS) for w, v in zip(halves(weights, downs), dy))
    pre_gate, pre_up = pre[:units], pre[units:]
    logistic = 1.0 / (1.0 + jnp.exp(-pre_gate))
    act = (pre_gate * logistic * pre_up).astype(jnp.bfloat16)
    d_s = jnp.sum(act.astype(jnp.float32) * d_act, axis=0, keepdims=True)
    d_gate = d_act * pre_up * logistic * (1.0 + pre_gate * (1.0 - logistic))
    d_up = d_act * pre_gate * logistic
    d_pre = jnp.concatenate([d_gate, d_up], axis=0)
    d_pre_low = d_pre.astype(jnp.bfloat16)
    if len(emits) == 1:
        ((send, factors),) = emits
        factors[gates] = d_pre_low
        factors[downs] = act
        send()
    else:
        for i, (send, grad) in enumerate(emits):
            grad[gates] = dot(d_pre_low, x[i], PLAIN).astype(grad.dtype)
            grad[downs] = dot(act, dy[i], PLAIN).astype(grad.dtype)
            send()
    return d_pre.T.astype(jnp.bfloat16), d_s


def far_body(width, units, fetches, near_in, emits, near_out):
    (wait_rows, rows_ref), weights = fetches[0], fetches[1:]
    wait_rows()
    send_rows, flat_ref = emits[2]
    flat_ref[...] = rows_ref[...].reshape(flat_ref.shape)
    send_rows()
    for wait, _ in weights:
        wait()
    refs = [ref for _, ref in weights]
    d_pre, d_s = block_grads(width, units, flat_ref, refs, emits[:2])
    near_out[0][...] = d_pre
    near_out[1][...] = jnp.broadcast_to(d_s, near_out[1].shape)


def rest_body(width, units, parts, fetches, near_in, emits, near_out):
    (wait_rows, rows_ref), weights = fetches[0], split_parts(parts, fetches[1:])
    count, half = len(parts), width // 2
    refs = [[ref for _, ref in pairs] for pairs in weights]
    wait_rows()
    d_pre, d_s = [near_in[0][...]], near_in[1][:1]
    for b in range(count):
        for wait, _ in weights[b]:
            wait()
        if b > 0:
            grads = emits[2 * (b - 1) : 2 * b] if b < count - 1 else emits[-2:-1]
            terms = block_grads(width, units, rows_ref, refs[b], grads)
            d_pre.append(terms[0])
            d_s = d_s + terms[1]
    send, out_ref = emits[-1]
    gates = slice(0, 2 * units)
    for i in range(2):
        total = sum(dot(d_pre[b], halves(refs[b], gates)[i], PLAIN) for b in range(count))
        total = total.astype(jnp.bfloat16).reshape((*out_ref.shape[:2], half))
        out_ref[:, :, i * half : (i + 1) * half] = total
    scores = jnp.broadcast_to(d_s, (LANES, d_s.shape[1])).T.astype(jnp.bfloat16)
    out_ref[:, :, width:] = scores.reshape((*out_ref.shape[:2], LANES))
    send()


def own_body(width, units, fetches, near_in, emits, near_out):
    (wait_rows, rows_ref), (wait_factors, factors) = fetches[:2]
    wait_rows()
    wait_factors()
    half, gates, downs = width // 2, slice(0, 2 * units), slice(2 * units, 3 * units)
    for i, (send, out) in enumerate(emits):
        wait, came = fetches[2 + i]
        wait()
        for rows, at in ((gates, 0), (downs, width)):
            side = rows_ref[:, at + i * half : at + (i + 1) * half]
            grad = dot(factors[rows], side, PLAIN) + came[rows].astype(jnp.float32)
            out[rows] = grad.astype(out.dtype)
        send()


def total_body(units, fetches, near_in, emits, near_out):
    half = fetches[0][1].shape[1]
    for i in range(2):
        pair = fetches[2 * i : 2 * i + 2]
        for wait, _ in pair:
            wait()
        for j, (send, out) in enumerate(emits):
            rows = slice(j * units, (j + 1) * units)
            out[:, i * half : (i + 1) * half] = sum(
                ref[rows].astype(jnp.float32) for _, ref in pair
            ).astype(jnp.bfloat16)
            if i == 1:
                send()


def matched(ids, expert_slots, k):
    return ids[k : k + 1] == expert_slots


def dispatch_body(ids_ref, scores_ref, tokens_ref, grad_ref, rows_ref, map_ref):
    slot_count, width = map_ref.shape[0], tokens_ref.shape[1]
    tok_count = tokens_ref.shape[0]
    shape = (slot_count, tok_count)
    slots = lax.broadcasted_iota(jnp.int32, shape, 0)
    ids, scores = ids_ref[...], scores_ref[...].astype(jnp.float32)
    named, weight = jnp.zeros(shape, jnp.float32), jnp.zeros(shape, jnp.float32)
    for k in range(TOP):
        hit = matched(ids, slots // CAP, k)
        named = jnp.where(hit, 1.0, named)
        weight = jnp.where(hit, scores[k : k + 1], weight)
    square = (tok_count, tok_count)
    earlier = lax.broadcasted_iota(jnp.int32, square, 0) < lax.broadcasted_iota(jnp.int32, square, 1)
    rank = dot(named.astype(jnp.bfloat16), earlier.astype(jnp.bfloat16), PLAIN)
    placed = jnp.where(rank == (slots % CAP).astype(jnp.float32), named, 0.0)
    slot_s = jnp.sum(placed * weight, axis=1, keepdims=True)
    token_map = placed.astype(jnp.bfloat16)
    map_ref[...] = token_map
    x = dot(token_map, tokens_ref[...], PLAIN).astype(jnp.bfloat16)
    rows_ref[:, :, :width] = x.reshape(slot_count // CAP, CAP, width)
    scaled = slot_s * dot(token_map, grad_ref[...], PLAIN)
    rows_ref[:, :, width:] = scaled.astype(jnp.bfloat16).reshape(slot_count // CAP, CAP, width)


def home_body(home_ref, ids_ref, scores_ref, map_ref, tokens_ref, out_scores_ref):
    width = tokens_ref.shape[1]
    token_map = map_ref[...]
    home = home_ref[...].reshape(token_map.shape[0], width + LANES)
    tokens_ref[...] = dot(token_map, home[:, :width], ROWS).astype(jnp.bfloat16)
    slots = lax.broadcasted_iota(jnp.int32, token_map.shape, 0)
    ids, scores = ids_ref[...], scores_ref[...].astype(jnp.float32)
    sums = token_map.astype(jnp.float32) * home[:, width : width + 1].astype(jnp.float32)
    for k in range(TOP):
        own = jnp.where(matched(ids, slots // CAP, k), sums, 0.0)
        total = jnp.sum(own, axis=0, keepdims=True) / scores[k : k + 1]
        out_scores_ref[k : k + 1] = total


def simple_call(body, outs, *operands):
    vmem = pl.BlockSpec(memory_space=pltpu.VMEM)
    size = sum(v.size * v.dtype.itemsize for v in (*operands, *outs))
    return pl.pallas_call(
        body,
        out_shape=outs,
        in_specs=[vmem] * len(operands),
        out_specs=[vmem] * len(outs),
        compiler_params=pltpu.CompilerParams(vmem_limit_bytes=16 << 20),
        cost_estimate=pl.CostEstimate(flops=0, bytes_accessed=size, transcendentals=0),
    )(*operands)


def on_device(tokens, grad_out, expert_ids, scores, gate_weight, up_weight, down_weight):
    ring = lax.axis_size("block")
    expert_count = lax.axis_size("node") * lax.axis_size("expert")
    tok_count, width = tokens.shape
    units = gate_weight.shape[2]
    half = width // 2
    slot_count = expert_count * CAP
    bf16, f32 = jnp.bfloat16, jnp.float32
    shape = jax.ShapeDtypeStruct

    matrices = [gate_weight[0, 0], up_weight[0, 0], down_weight[0, 0]]
    own_a = jnp.concatenate([w[:, :half] for w in matrices], axis=0)
    own_b = jnp.concatenate([w[:, half:] for w in matrices], axis=0)
    before_a, after_b = hold(right(own_a, ring)), hold(left(own_b, ring))
    before = (before_a, right(own_b, ring))
    after = (left(own_a, ring), after_b)
    far_a, far_b = right(before_a, ring), left(after_b, ring)

    ids_t, scores_t = expert_ids.T, scores.T
    outgoing, token_map = simple_call(
        dispatch_body,
        [shape((expert_count, CAP, 2 * width), bf16), shape((slot_count, tok_count), bf16)],
        ids_t,
        scores_t,
        tokens,
        grad_out,
    )
    rows = lax.all_to_all(
        outgoing, ("node", "expert"), 0, 0, tiled=True
    )
    half_grad = shape((3 * units, half), bf16)
    block_flops = 12 * slot_count * units * width

    far_grad_a, far_grad_b, flat_rows, far_pre, far_s = on_core(
        functools.partial(far_body, width, units),
        [rows, far_a, far_b],
        [],
        [half_grad, half_grad, shape((slot_count, 2 * width), bf16)],
        [shape((slot_count, 2 * units), bf16), shape((SUBLANES, slot_count), f32)],
        block_flops,
    )
    passing_a = right(far_grad_a, ring)
    passing_b = left(far_grad_b, ring)
    nxt_a, nxt_b, prev_a, prev_b, factors, returning = on_core(
        functools.partial(rest_body, width, units, [2] * ring),
        [flat_rows, far_a, far_b, *after, *before, own_a, own_b],
        [far_pre, far_s],
        [half_grad] * 4
        + [
            shape((3 * units, slot_count), bf16),
            shape((expert_count, CAP, width + LANES), bf16),
        ],
        [],
        4 * block_flops,
    )
    left_b = right(nxt_b, ring)
    right_a = left(prev_a, ring)
    left_a = right((nxt_a.astype(f32) + passing_a.astype(f32)).astype(bf16), ring)
    right_b = left((prev_b.astype(f32) + passing_b.astype(f32)).astype(bf16), ring)
    part_a, part_b = on_core(
        functools.partial(own_body, width, units),
        [flat_rows, factors, right_a, left_b],
        [],
        [half_grad, half_grad],
        [],
        FLOPS_PART,
    )
    d_gate, d_up, d_down = on_core(
        functools.partial(total_body, units),
        [part_a, left_a, part_b, right_b],
        [],
        [shape((units, width), bf16)] * 3,
        [],
        0,
    )

    home = lax.all_to_all(
        returning, ("node", "expert"), 0, 0, tiled=True
    )
    d_tokens, d_scores_t = simple_call(
        home_body,
        [shape((tok_count, width), bf16), shape((TOP, tok_count), f32)],
        home,
        ids_t,
        scores_t,
        token_map,
    )
    d_scores = d_scores_t.T.astype(bf16)
    return (d_tokens, d_scores, d_gate[None, None], d_up[None, None], d_down[None, None])


def solution(mesh):
    node_count, local_count = mesh.devices.shape
    mesh = Mesh(
        mesh.devices.reshape(node_count, EXP_NODE, local_count // EXP_NODE),
        ("node", "expert", "block"),
    )
    by_token = P(("node", "expert", "block"), None)
    by_block = P("node", ("expert", "block"), None, None)
    return jax.shard_map(
        on_device,
        mesh=mesh,
        in_specs=(by_token,) * 4 + (by_block,) * 3,
        out_specs=(by_token,) * 2 + (by_block,) * 3,
        check_vma=False,
    )
```
